32 devices in a mesh: replica: 4 (over y, x), fsdp: 8 (over z, core).
Axes of the slice: x: 2, y: 2, z: 4, core: 2. Of those that a mesh axis runs over, the one named last changes fastest.
Arguments:
- inputs: bfloat16 [8192, 4096], P(('replica', 'fsdp')), may hold values from -100 to 100
- out_grad: bfloat16 [8192, 512], P(('replica', 'fsdp')), may hold values from -1 to 1
- inner_weight: float32 [4, 4096, 512], P('replica', 'fsdp'), may hold values from -0.6 to 0.6
- adam_first: float32 [4, 4096, 512], P('replica', 'fsdp'), may hold values from -1.8 to 1.8
- adam_second: float32 [4, 4096, 512], P('replica', 'fsdp'), may hold values from 0.05 to 1
- fragment_local: float32 [4, 2, 8192, 1024], P('replica', None, 'fsdp'), may hold values from -3 to 3
- anchor: float32 [2, 8192, 1024], P(None, 'fsdp'), may hold values from -3 to 3
- outer_momentum: float32 [2, 8192, 1024], P(None, 'fsdp'), may hold values from -1.8 to 1.8
- outer_prev: float32 [2, 8192, 1024], P(None, 'fsdp'), may hold values from -1.8 to 1.8
Outputs:
- new_weight: float32 [4, 4096, 512], P('replica', 'fsdp')
- new_first: float32 [4, 4096, 512], P('replica', 'fsdp')
- new_second: float32 [4, 4096, 512], P('replica', 'fsdp')
- outer_delta: float32 [2, 8192, 1024], P(None, 'fsdp')
- new_momentum: float32 [2, 8192, 1024], P(None, 'fsdp')
- new_anchor: float32 [2, 8192, 1024], P(None, 'fsdp')
The draws below stay inside these ranges and needn't reach their ends.
All inputs are finite; a program needn't handle non-finite values.
Results may differ from the reference program's by a relative error of at most 0.0003.
Values may be sent and summed in bfloat16 or wider, within the bound.
A program may use at most 192 MiB of HBM per device.

```python
import math
import jax
import jax.numpy as jnp
from jax import lax

D = 8192
KV = 1024
DW = 4096
KW = 512
FL = 2
TOK_DEV = 256
TOKENS = 8192
N_REPLICA = 4
N_FSDP = 8


def draw_inputs(key, part):
    key = jax.random.fold_in(key, 11)
    key_base, key_cols, key_rows = jax.random.split(key, 3)
    ramp = 3.0 ** (jnp.arange(DW, dtype=jnp.float32) / (DW - 1))
    col_scale = jnp.exp(jax.random.uniform(key_cols, (DW,), jnp.float32, 0.0, math.log(10.0)))
    row_scale = jnp.exp(jax.random.uniform(key_rows, (TOKENS, 1), jnp.float32, 0.0, math.log(10.0)))
    base = jnp.clip(jax.random.normal(key_base, (TOKENS, DW), jnp.float32), -6.0, 6.0)
    values = jnp.clip(0.1 * base * ramp * col_scale * row_scale, -100.0, 100.0)
    return values.astype(jnp.bfloat16)


def draw_out_grad(key, part):
    key = jax.random.fold_in(key, 23)
    key_base, key_order = jax.random.split(key)
    per_replica = TOKENS // N_REPLICA
    rungs = max(N_REPLICA - 1, 1)
    placing = jax.random.permutation(key_order, N_REPLICA).astype(jnp.float32)
    level = 0.4 * 2.0 ** (-8.0 * placing / rungs)
    row_level = jnp.repeat(level, per_replica)[:, None]
    base = jnp.clip(jax.random.normal(key_base, (TOKENS, KW), jnp.float32), -2.5, 2.5)
    return (base * row_level).astype(jnp.bfloat16)


def block_scale(rng, dims, shards, low, top_value):
    loudness = 1.0
    for dim, parts in shards:
        heights = jax.random.uniform(jax.random.fold_in(jax.random.fold_in(rng, 6), dim), (parts,), jnp.float32, low / len(shards), top_value / len(shards))
        loudness = loudness * jnp.repeat(jnp.exp(heights), dims[dim] // parts).reshape((-1,) + (1,) * (len(dims) - 1 - dim))
    return loudness


def scatter_about(rng, dims, width, limit, pieces=(), kind=jnp.bfloat16):
    array = jax.random.normal(rng, dims, jnp.float32) * width
    if len(pieces) > 0:
        array = block_scale(rng, dims, pieces, -0.22, 0.18) * array
    return jnp.clip(array, min=-limit, max=limit).astype(kind)


def setup_inputs(seed: int = 0) -> dict:
    seeds = jax.random.split(jax.random.key(seed), 10)
    inputs = draw_inputs(jax.random.fold_in(seeds[9], 71), 0)
    out_grad = draw_out_grad(jax.random.fold_in(seeds[9], 71), 0)
    inner_weight = scatter_about(seeds[2], (N_REPLICA, DW, KW), 0.1, 0.6, ((0, 4), (1, 8)), jnp.float32)
    adam_first = scatter_about(seeds[3], (N_REPLICA, DW, KW), 0.3, 1.8, ((0, 4), (1, 8)), jnp.float32)
    adam_second = jnp.clip(jnp.exp(math.log(1.0) - 2.9957323 * jax.random.uniform(seeds[4], (N_REPLICA, DW, KW), jnp.float32) ** block_scale(seeds[4], (N_REPLICA, DW, KW), ((0, 4), (1, 8)), -0.2, 0.2)), 0.05, 1.0)
    fragment_local = scatter_about(seeds[5], (N_REPLICA, FL, D, KV), 0.5, 3.0, ((0, 4), (2, 8)), jnp.float32)
    anchor = scatter_about(seeds[6], (FL, D, KV), 0.5, 3.0, ((1, 8),), jnp.float32)
    outer_momentum = scatter_about(seeds[7], (FL, D, KV), 0.3, 1.8, ((1, 8),), jnp.float32)
    outer_prev = scatter_about(seeds[8], (FL, D, KV), 0.3, 1.8, ((1, 8),), jnp.float32)
    return {"inputs": inputs, "out_grad": out_grad, "inner_weight": inner_weight, "adam_first": adam_first, "adam_second": adam_second, "fragment_local": fragment_local, "anchor": anchor, "outer_momentum": outer_momentum, "outer_prev": outer_prev}


first_decay = 0.9
second_decay = 0.95
inner_rate = 0.02
outer_rate = 0.7
outer_mu = 0.9
clip_rms = 4.0
adam_eps = 1e-08
norm_eps = 1e-06

def replica_grad(operands):
    activations, token_grads = operands
    return lax.dot_general(activations, token_grads, (((0,), (0,)), ((), ())), preferred_element_type=jnp.float32)

def reference(inputs, out_grad, inner_weight, adam_first, adam_second, fragment_local, anchor, outer_momentum, outer_prev):
    per_replica = TOK_DEV * N_FSDP
    activations = inputs.reshape(N_REPLICA, per_replica, DW)
    token_grads = out_grad.reshape(N_REPLICA, per_replica, KW)
    weight_grad = lax.map(replica_grad, (activations, token_grads))
    norm_sq = lax.optimization_barrier(jnp.sum(weight_grad * weight_grad, axis=(1, 2), keepdims=True))
    clip_limit = clip_rms * math.sqrt(DW * KW)
    factor = jnp.minimum(1.0, clip_limit / jnp.sqrt(norm_sq + norm_eps))
    clipped = weight_grad * factor
    new_first = first_decay * adam_first + (1.0 - first_decay) * clipped
    new_second = second_decay * adam_second + (1.0 - second_decay) * clipped * clipped
    new_weight = inner_weight - inner_rate * new_first / (jnp.sqrt(new_second) + adam_eps)
    outer_delta = lax.optimization_barrier(jnp.sum(anchor[None] - fragment_local, axis=0)) / N_REPLICA
    new_momentum = outer_mu * outer_momentum + outer_prev
    new_anchor = anchor - outer_rate * (outer_prev + outer_mu * new_momentum)
    return (new_weight, new_first, new_second, outer_delta, new_momentum, new_anchor)
```

```python
import functools
import math

import jax
import jax.numpy as jnp
from jax import lax
from jax.experimental import pallas as pl
from jax.experimental.pallas import tpu as pltpu
from jax.sharding import PartitionSpec as P

first_decay = 0.9
second_decay = 0.95
inner_rate = 0.02
outer_rate = 0.7
outer_mu = 0.9
clip_rms = 4.0
adam_eps = 1e-08
norm_eps = 1e-06


KIND_A, KIND_B, KIND_C, KIND_G0, KIND_G1, KIND_F = range(6)
SPAN = 172.0
HALF_SPAN = 86.0
PIECES = 2
STEP_ROWS = 32


def outer_kernel(rows, width, local_ref, anchor_ref, out_ref, vf, va, sent, held, load_sem, store_sem, send_sem, recv_sem):
    me = lax.axis_index("replica")
    ny = (me + 2) % 4
    nx = 3 - ny
    diag = 3 - me
    neighbour = (nx, ny)
    owners = (diag, nx, ny, me)
    steps = rows // STEP_ROWS

    loads = []
    for j in range(4):
        part = pl.ds(pl.multiple_of(owners[j] * rows, rows), rows)
        loads.append(
            (
                pltpu.make_async_copy(local_ref.at[part, :], vf.at[j], load_sem.at[j, 0]),
                pltpu.make_async_copy(anchor_ref.at[part, :], va.at[j], load_sem.at[j, 1]),
            )
        )
    for pair in loads:
        for load in pair:
            load.start()

    barrier = pltpu.get_barrier_semaphore()
    for n in neighbour:
        pl.semaphore_signal(barrier, inc=1, device_id={"replica": n}, device_id_type=pl.DeviceIdType.MESH)
    pl.semaphore_wait(barrier, 2)

    def columns(half, k):
        return pl.ds((half * PIECES + k) * width, width)

    def copy(kind, way, k):
        if kind == KIND_F:
            src = held.at[KIND_G1 if way == 0 else KIND_G0, 1 - way, k]
        elif kind in (KIND_G0, KIND_G1):
            src = sent.at[kind, 0, k]
        else:
            src = sent.at[kind, way, k]
        return pltpu.make_async_remote_copy(
            src_ref=src,
            dst_ref=held.at[kind, way, k],
            send_sem=send_sem.at[kind, way, k],
            recv_sem=recv_sem.at[kind, way, k],
            device_id={"replica": neighbour[way]},
            device_id_type=pl.DeviceIdType.MESH,
        )

    def scale_of(box, kind, way, k):
        return box[kind, way, k, rows : rows + 16, :].astype(jnp.float32)[0:1] * (1.0 / SPAN)

    def decoded(box, kind, way, k, scale, r):
        code = box[kind, way, k, r, :].astype(jnp.float32)
        size = (jnp.log(jnp.abs(code)) + HALF_SPAN) * scale
        return jnp.where(code < 0.0, -size, size)

    def encode(j, half, k, kind, way, terms, factor=None):
        cs = columns(half, k)
        scales = [scale_of(held, t[0], t[1], k) for t in terms]

        def gather(i, top):
            r = pl.ds(pl.multiple_of(i * STEP_ROWS, STEP_ROWS), STEP_ROWS)
            x = va[j, r, cs] - vf[j, r, cs]
            for t, s in zip(terms, scales):
                x = x + decoded(held, t[0], t[1], k, s, r)
            if factor is not None:
                x = x * factor
            vf[j, r, cs] = x
            return jnp.maximum(top, jnp.max(jnp.abs(x).reshape(STEP_ROWS // 8, 8, width), axis=0))

        top = lax.fori_loop(0, steps, gather, jnp.zeros((8, width), jnp.float32))
        top = (jnp.max(top, axis=0, keepdims=True) * 1.01 + 1e-30).astype(jnp.bfloat16)
        sent[kind, way, k, rows : rows + 16, :] = jnp.broadcast_to(top.astype(jnp.float32), (16, width)).astype(
            jnp.bfloat16
        )
        slope = SPAN / top.astype(jnp.float32)

        def write(i, c):
            r = pl.ds(pl.multiple_of(i * STEP_ROWS, STEP_ROWS), STEP_ROWS)
            x = vf[j, r, cs]
            y = jnp.exp(jnp.abs(x) * slope - HALF_SPAN)
            sent[kind, way, k, r, :] = jnp.where(x < 0.0, -y, y).astype(jnp.bfloat16)
            return c

        lax.fori_loop(0, steps, write, 0)

    def unfold(j, half, k, box, kind, way):
        cs = columns(half, k)
        scale = scale_of(box, kind, way, k)

        def step(i, c):
            r = pl.ds(pl.multiple_of(i * STEP_ROWS, STEP_ROWS), STEP_ROWS)
            vf[j, r, cs] = decoded(box, kind, way, k, scale, r)
            return c

        lax.fori_loop(0, steps, step, 0)

    def loaded(j):
        for load in loads[j]:
            load.wait()

    loaded(0)
    for k in range(PIECES):
        for way in (0, 1):
            encode(0, 1 - way, k, KIND_A, way, ())
            copy(KIND_A, way, k).start()
    loaded(1)
    loaded(2)
    for k in range(PIECES):
        for way in (0, 1):
            encode(1 + way, 1 - way, k, KIND_B, way, ())
            copy(KIND_B, way, k).start()
    for k in range(PIECES):
        for way in (0, 1):
            copy(KIND_A, 1 - way, k).wait_recv()
            encode(1 + way, way, k, KIND_C, way, ((KIND_A, 1 - way),))
            copy(KIND_C, way, k).start()
    loaded(3)
    for k in range(PIECES):
        for half in (0, 1):
            copy(KIND_B, 1 - half, k).wait_recv()
            copy(KIND_C, half, k).wait_recv()
            encode(3, half, k, KIND_G0 + half, 0, ((KIND_B, 1 - half), (KIND_C, half)), 0.25)
            for way in (0, 1):
                copy(KIND_G0 + half, way, k).start()

    def store(j):
        part = pl.ds(pl.multiple_of(owners[j] * rows, rows), rows)
        return pltpu.make_async_copy(vf.at[j], out_ref.at[part, :], store_sem.at[j])

    for k in range(PIECES):
        for half in (0, 1):
            unfold(3, half, k, sent, KIND_G0 + half, 0)
    store(3).start()
    for k in range(PIECES):
        for way in (0, 1):
            first = KIND_G1 if way == 0 else KIND_G0
            copy(first, 1 - way, k).wait_recv()
            copy(KIND_F, way, k).start()
    for k in range(PIECES):
        for way in (0, 1):
            unfold(1 + way, way, k, held, KIND_G0 + way, way)
    for way in (0, 1):
        for k in range(PIECES):
            late = 1 - way
            copy(KIND_G0 + late, way, k).wait_recv()
            unfold(1 + way, late, k, held, KIND_G0 + late, way)
        store(1 + way).start()
    for k in range(PIECES):
        for way in (0, 1):
            copy(KIND_F, way, k).wait_recv()
            unfold(0, 1 - way, k, held, KIND_F, way)
    store(0).start()
    for kind in range(6):
        for way in (0, 1):
            for k in range(PIECES):
                copy(kind, way, k).wait_send()
    for j in range(4):
        store(j).wait()


def outer_mean(anchor, fragment_local):
    replicas = lax.axis_size("replica")
    layers, depth, width = anchor.shape
    rows = layers * depth // 4
    piece = width // (2 * PIECES)
    if replicas != 4 or (layers * depth) % (4 * STEP_ROWS) != 0 or width % (256 * PIECES) != 0:
        spread = anchor - fragment_local[0]
        return lax.psum(spread, "replica") / replicas
    sems = pltpu.SemaphoreType.DMA
    mean = pl.pallas_call(
        functools.partial(outer_kernel, rows, piece),
        out_shape=jax.ShapeDtypeStruct((4 * rows, width), jnp.float32),
        in_specs=[pl.BlockSpec(memory_space=pl.ANY)] * 2,
        out_specs=pl.BlockSpec(memory_space=pl.ANY),
        scratch_shapes=[
            pltpu.VMEM((4, rows, width), jnp.float32),
            pltpu.VMEM((4, rows, width), jnp.float32),
            pltpu.VMEM((5, 2, PIECES, rows + 16, piece), jnp.bfloat16),
            pltpu.VMEM((6, 2, PIECES, rows + 16, piece), jnp.bfloat16),
            sems((4, 2)),
            sems((4,)),
            sems((6, 2, PIECES)),
            sems((6, 2, PIECES)),
        ],
        compiler_params=pltpu.CompilerParams(
            collective_id=0, has_side_effects=True, vmem_limit_bytes=48 * 1024 * 1024
        ),
        cost_estimate=pl.CostEstimate(
            flops=40 * layers * depth * width, bytes_accessed=12 * layers * depth * width, transcendentals=0
        ),
    )(fragment_local.reshape(4 * rows, width), anchor.reshape(4 * rows, width))
    return mean.reshape(anchor.shape)


def body(
    inputs,
    out_grad,
    inner_weight,
    adam_first,
    adam_second,
    fragment_local,
    anchor,
    outer_momentum,
    outer_prev,
):
    groups = lax.axis_size("fsdp")
    feature_rows = inner_weight.shape[1]
    out_features = inner_weight.shape[2]
    grad_shard = lax.psum_scatter(
        lax.dot_general(
            inputs, out_grad, (((0,), (0,)), ((), ())), preferred_element_type=jnp.float32
        ),
        "fsdp",
        scatter_dimension=0,
        tiled=True,
    )
    norm_sq = lax.psum(jnp.sum(grad_shard * grad_shard), "fsdp")
    clip_limit = clip_rms * math.sqrt(feature_rows * groups * out_features)
    factor = jnp.minimum(1.0, clip_limit / jnp.sqrt(norm_sq + norm_eps))
    clipped = (grad_shard * factor)[None]
    new_first = first_decay * adam_first + (1.0 - first_decay) * clipped
    new_second = second_decay * adam_second + (1.0 - second_decay) * clipped * clipped
    new_weight = inner_weight - inner_rate * new_first / (jnp.sqrt(new_second) + adam_eps)
    new_momentum = outer_mu * outer_momentum + outer_prev
    new_anchor = anchor - outer_rate * (outer_prev + outer_mu * new_momentum)
    outer_delta = outer_mean(anchor, fragment_local)
    return (new_weight, new_first, new_second, outer_delta, new_momentum, new_anchor)


def solution(mesh):
    placed = (
        P(("replica", "fsdp"), None),
        P(("replica", "fsdp"), None),
        P("replica", "fsdp", None),
        P("replica", "fsdp", None),
        P("replica", "fsdp", None),
        P("replica", None, "fsdp", None),
        P(None, "fsdp", None),
        P(None, "fsdp", None),
        P(None, "fsdp", None),
    )
    return jax.shard_map(
        body,
        mesh=mesh,
        in_specs=placed,
        out_specs=(
            P("replica", "fsdp", None),
            P("replica", "fsdp", None),
            P("replica", "fsdp", None),
            P(None, "fsdp", None),
            P(None, "fsdp", None),
            P(None, "fsdp", None),
        ),
        check_vma=False,
    )
```

```python
import functools
import math

import jax
import jax.numpy as jnp
from jax import lax
from jax.experimental import pallas as pl
from jax.experimental.pallas import tpu as pltpu
from jax.sharding import PartitionSpec as P

first_decay = 0.9
second_decay = 0.95
inner_rate = 0.02
outer_rate = 0.7
outer_mu = 0.9
clip_rms = 4.0
adam_eps = 1e-08
norm_eps = 1e-06


KIND_A, KIND_B, KIND_C, KIND_G0, KIND_G1, KIND_F = range(6)
SPAN = 172.0
HALF_SPAN = 86.0
PIECES = 2
STEP_ROWS = 32


def outer_kernel(
    rows,
    width,
    group,
    local_ref,
    anchor_ref,
    grad_ref,
    out_ref,
    shard_ref,
    norm_ref,
    vf,
    va,
    sent,
    held,
    load_sem,
    store_sem,
    send_sem,
    recv_sem,
    own,
    twin,
    grad_sent,
    grad_held,
    part_sent,
    part_held,
    own_sem,
    twin_sem,
    grad_sem,
    part_sem,
):
    me = lax.axis_index("replica")
    ny = (me + 2) % 4
    nx = 3 - ny
    diag = 3 - me
    neighbour = (nx, ny)
    owners = (diag, nx, ny, me)
    steps = rows // STEP_ROWS

    place = lax.axis_index("fsdp")
    core = place % 2
    chip = place // 2
    chips = group // 2
    block = shard_ref.shape[0]
    grad_steps = block // STEP_ROWS

    def own_copy(s):
        start = pl.multiple_of((((chip + s) % chips) * 2 + core) * block, block)
        return pltpu.make_async_copy(grad_ref.at[pl.ds(start, block), :], own.at[s], own_sem.at[s])

    def twin_copy(s):
        start = pl.multiple_of((((chip + s) % chips) * 2 + 1 - core) * block, block)
        return pltpu.make_async_remote_copy(
            src_ref=grad_ref.at[pl.ds(start, block), :],
            dst_ref=twin.at[s],
            send_sem=twin_sem.at[0, s],
            recv_sem=twin_sem.at[1, s],
            device_id={"fsdp": chip * 2 + 1 - core},
            device_id_type=pl.DeviceIdType.MESH,
        )

    def grad_copy(s):
        return pltpu.make_async_remote_copy(
            src_ref=grad_sent.at[s - 1],
            dst_ref=grad_held.at[s - 1],
            send_sem=grad_sem.at[0, s - 1],
            recv_sem=grad_sem.at[1, s - 1],
            device_id={"fsdp": ((chip + s) % chips) * 2 + core},
            device_id_type=pl.DeviceIdType.MESH,
        )

    def part_copy(s):
        return pltpu.make_async_remote_copy(
            src_ref=part_sent,
            dst_ref=part_held.at[s - 1],
            send_sem=part_sem.at[0, s - 1],
            recv_sem=part_sem.at[1, s - 1],
            device_id={"fsdp": (place + s) % group},
            device_id_type=pl.DeviceIdType.MESH,
        )

    loads = []
    for j in range(4):
        part = pl.ds(pl.multiple_of(owners[j] * rows, rows), rows)
        loads.append(
            (
                pltpu.make_async_copy(local_ref.at[part, :], vf.at[j], load_sem.at[j, 0]),
                pltpu.make_async_copy(anchor_ref.at[part, :], va.at[j], load_sem.at[j, 1]),
            )
        )
    for pair in loads:
        for load in pair:
            load.start()

    barrier = pltpu.get_barrier_semaphore()
    for n in neighbour:
        pl.semaphore_signal(barrier, inc=1, device_id={"replica": n}, device_id_type=pl.DeviceIdType.MESH)
    for s in range(1, group):
        pl.semaphore_signal(
            barrier, inc=1, device_id={"fsdp": (place + s) % group}, device_id_type=pl.DeviceIdType.MESH
        )
    pl.semaphore_wait(barrier, group + 1)

    for s in range(chips):
        own_copy(s).start()
        twin_copy(s).start()

    def columns(half, k):
        return pl.ds((half * PIECES + k) * width, width)

    def copy(kind, way, k):
        if kind == KIND_F:
            src = held.at[KIND_G1 if way == 0 else KIND_G0, 1 - way, k]
        elif kind in (KIND_G0, KIND_G1):
            src = sent.at[kind, 0, k]
        else:
            src = sent.at[kind, way, k]
        return pltpu.make_async_remote_copy(
            src_ref=src,
            dst_ref=held.at[kind, way, k],
            send_sem=send_sem.at[kind, way, k],
            recv_sem=recv_sem.at[kind, way, k],
            device_id={"replica": neighbour[way]},
            device_id_type=pl.DeviceIdType.MESH,
        )

    def scale_of(box, kind, way, k):
        return box[kind, way, k, rows : rows + 16, :].astype(jnp.float32)[0:1] * (1.0 / SPAN)

    def decoded(box, kind, way, k, scale, r):
        code = box[kind, way, k, r, :].astype(jnp.float32)
        size = (jnp.log(jnp.abs(code)) + HALF_SPAN) * scale
        return jnp.where(code < 0.0, -size, size)

    def encode(j, half, k, kind, way, terms, factor=None):
        cs = columns(half, k)
        scales = [scale_of(held, t[0], t[1], k) for t in terms]

        def gather(i, top):
            r = pl.ds(pl.multiple_of(i * STEP_ROWS, STEP_ROWS), STEP_ROWS)
            x = va[j, r, cs] - vf[j, r, cs]
            for t, s in zip(terms, scales):
                x = x + decoded(held, t[0], t[1], k, s, r)
            if factor is not None:
                x = x * factor
            vf[j, r, cs] = x
            return jnp.maximum(top, jnp.max(jnp.abs(x).reshape(STEP_ROWS // 8, 8, width), axis=0))

        top = lax.fori_loop(0, steps, gather, jnp.zeros((8, width), jnp.float32))
        top = (jnp.max(top, axis=0, keepdims=True) * 1.01 + 1e-30).astype(jnp.bfloat16)
        sent[kind, way, k, rows : rows + 16, :] = jnp.broadcast_to(top.astype(jnp.float32), (16, width)).astype(
            jnp.bfloat16
        )
        slope = SPAN / top.astype(jnp.float32)

        def write(i, c):
            r = pl.ds(pl.multiple_of(i * STEP_ROWS, STEP_ROWS), STEP_ROWS)
            x = vf[j, r, cs]
            y = jnp.exp(jnp.abs(x) * slope - HALF_SPAN)
            sent[kind, way, k, r, :] = jnp.where(x < 0.0, -y, y).astype(jnp.bfloat16)
            return c

        lax.fori_loop(0, steps, write, 0)

    def unfold(j, half, k, box, kind, way):
        cs = columns(half, k)
        scale = scale_of(box, kind, way, k)

        def step(i, c):
            r = pl.ds(pl.multiple_of(i * STEP_ROWS, STEP_ROWS), STEP_ROWS)
            vf[j, r, cs] = decoded(box, kind, way, k, scale, r)
            return c

        lax.fori_loop(0, steps, step, 0)

    def loaded(j):
        for load in loads[j]:
            load.wait()

    def encode_grad(s):
        span = own.shape[2]

        def gather(i, top):
            r = pl.ds(pl.multiple_of(i * STEP_ROWS, STEP_ROWS), STEP_ROWS)
            x = own[s, r, :] + twin[s, r, :]
            own[s, r, :] = x
            return jnp.maximum(top, jnp.max(jnp.abs(x).reshape(STEP_ROWS // 8, 8, span), axis=0))

        top = lax.fori_loop(0, grad_steps, gather, jnp.zeros((8, span), jnp.float32))
        top = (jnp.max(top, axis=0, keepdims=True) * 1.01 + 1e-30).astype(jnp.bfloat16).astype(jnp.float32)
        grad_sent[s - 1, block : block + 16, :] = jnp.broadcast_to(top, (16, span)).astype(jnp.bfloat16)
        slope = SPAN / top

        def write(i, c):
            r = pl.ds(pl.multiple_of(i * STEP_ROWS, STEP_ROWS), STEP_ROWS)
            x = own[s, r, :]
            y = jnp.exp(jnp.abs(x) * slope - HALF_SPAN)
            grad_sent[s - 1, r, :] = jnp.where(x < 0.0, -y, y).astype(jnp.bfloat16)
            return c

        lax.fori_loop(0, grad_steps, write, 0)

    def reduce_grad():
        span = own.shape[2]
        scales = [
            grad_held[s - 1, block : block + 16, :].astype(jnp.float32)[0:1] * (1.0 / SPAN)
            for s in range(1, chips)
        ]

        def step(i, squares):
            r = pl.ds(pl.multiple_of(i * STEP_ROWS, STEP_ROWS), STEP_ROWS)
            x = own[0, r, :] + twin[0, r, :]
            for s in range(1, chips):
                code = grad_held[s - 1, r, :].astype(jnp.float32)
                size = (jnp.log(jnp.abs(code)) + HALF_SPAN) * scales[s - 1]
                x = x + jnp.where(code < 0.0, -size, size)
            own[0, r, :] = x
            return squares + jnp.sum((x * x).reshape(STEP_ROWS // 8, 8, span), axis=0)

        squares = lax.fori_loop(0, grad_steps, step, jnp.zeros((8, span), jnp.float32))
        total = squares[:, 0:128]
        for c in range(1, span // 128):
            total = total + squares[:, c * 128 : (c + 1) * 128]
        part_sent[...] = total

    loaded(0)
    for k in range(PIECES):
        for way in (0, 1):
            encode(0, 1 - way, k, KIND_A, way, ())
            copy(KIND_A, way, k).start()
    loaded(1)
    loaded(2)
    for k in range(PIECES):
        for way in (0, 1):
            encode(1 + way, 1 - way, k, KIND_B, way, ())
            copy(KIND_B, way, k).start()
    for s in (2, 1, 3) if chips == 4 else range(1, chips):
        own_copy(s).wait()
        twin_copy(s).wait_recv()
        encode_grad(s)
        grad_copy(s).start()
    for k in range(PIECES):
        for way in (0, 1):
            copy(KIND_A, 1 - way, k).wait_recv()
            encode(1 + way, way, k, KIND_C, way, ((KIND_A, 1 - way),))
            copy(KIND_C, way, k).start()
    loaded(3)
    for k in range(PIECES):
        for half in (0, 1):
            copy(KIND_B, 1 - half, k).wait_recv()
            copy(KIND_C, half, k).wait_recv()
            encode(3, half, k, KIND_G0 + half, 0, ((KIND_B, 1 - half), (KIND_C, half)), 0.25)
            for way in (0, 1):
                copy(KIND_G0 + half, way, k).start()

    own_copy(0).wait()
    twin_copy(0).wait_recv()
    for s in range(1, chips):
        grad_copy(s).wait_recv()
    reduce_grad()
    for s in range(1, group):
        part_copy(s).start()
    shard_store = pltpu.make_async_copy(own.at[0], shard_ref, own_sem.at[0])
    shard_store.start()

    def store(j):
        part = pl.ds(pl.multiple_of(owners[j] * rows, rows), rows)
        return pltpu.make_async_copy(vf.at[j], out_ref.at[part, :], store_sem.at[j])

    for k in range(PIECES):
        for half in (0, 1):
            unfold(3, half, k, sent, KIND_G0 + half, 0)
    store(3).start()
    for k in range(PIECES):
        for way in (0, 1):
            first = KIND_G1 if way == 0 else KIND_G0
            copy(first, 1 - way, k).wait_recv()
            copy(KIND_F, way, k).start()
    for k in range(PIECES):
        for way in (0, 1):
            unfold(1 + way, way, k, held, KIND_G0 + way, way)
    for way in (0, 1):
        for k in range(PIECES):
            late = 1 - way
            copy(KIND_G0 + late, way, k).wait_recv()
            unfold(1 + way, late, k, held, KIND_G0 + late, way)
        store(1 + way).start()
    for k in range(PIECES):
        for way in (0, 1):
            copy(KIND_F, way, k).wait_recv()
            unfold(0, 1 - way, k, held, KIND_F, way)
    store(0).start()
    norm = part_sent[...]
    for s in range(1, group):
        part_copy(s).wait_recv()
        norm = norm + part_held[s - 1]
    norm_ref[...] = norm
    shard_store.wait()
    for s in range(chips):
        twin_copy(s).wait_send()
    for s in range(1, chips):
        grad_copy(s).wait_send()
    for s in range(1, group):
        part_copy(s).wait_send()
    for kind in range(6):
        for way in (0, 1):
            for k in range(PIECES):
                copy(kind, way, k).wait_send()
    for j in range(4):
        store(j).wait()


def fits(anchor, grad, feature_rows):
    layers, depth, width = anchor.shape
    return (
        lax.axis_size("replica") == 4
        and (layers * depth) % (4 * STEP_ROWS) == 0
        and width % (256 * PIECES) == 0
        and lax.axis_size("fsdp") == 8
        and feature_rows % STEP_ROWS == 0
        and grad.shape[1] % 128 == 0
        and layers * depth * width <= 2 * 1024 * 1024
    )


def joint_sums(anchor, fragment_local, grad, feature_rows):
    layers, depth, width = anchor.shape
    group = lax.axis_size("fsdp")
    chips = group // 2
    rows = layers * depth // 4
    piece = width // (2 * PIECES)
    out_features = grad.shape[1]
    sems = pltpu.SemaphoreType.DMA
    return pl.pallas_call(
        functools.partial(outer_kernel, rows, piece, group),
        out_shape=(
            jax.ShapeDtypeStruct((4 * rows, width), jnp.float32),
            jax.ShapeDtypeStruct((feature_rows, out_features), jnp.float32),
            jax.ShapeDtypeStruct((8, 128), jnp.float32),
        ),
        in_specs=[pl.BlockSpec(memory_space=pl.ANY)] * 3,
        out_specs=(
            pl.BlockSpec(memory_space=pl.ANY),
            pl.BlockSpec(memory_space=pl.ANY),
            pl.BlockSpec(memory_space=pltpu.VMEM),
        ),
        scratch_shapes=[
            pltpu.VMEM((4, rows, width), jnp.float32),
            pltpu.VMEM((4, rows, width), jnp.float32),
            pltpu.VMEM((5, 2, PIECES, rows + 16, piece), jnp.bfloat16),
            pltpu.VMEM((6, 2, PIECES, rows + 16, piece), jnp.bfloat16),
            sems((4, 2)),
            sems((4,)),
            sems((6, 2, PIECES)),
            sems((6, 2, PIECES)),
            pltpu.VMEM((chips, feature_rows, out_features), jnp.float32),
            pltpu.VMEM((chips, feature_rows, out_features), jnp.float32),
            pltpu.VMEM((chips - 1, feature_rows + 16, out_features), jnp.bfloat16),
            pltpu.VMEM((chips - 1, feature_rows + 16, out_features), jnp.bfloat16),
            pltpu.VMEM((8, 128), jnp.float32),
            pltpu.VMEM((group - 1, 8, 128), jnp.float32),
            sems((chips,)),
            sems((2, chips)),
            sems((2, chips - 1)),
            sems((2, group - 1)),
        ],
        compiler_params=pltpu.CompilerParams(
            collective_id=0, has_side_effects=True, vmem_limit_bytes=50 * 1024 * 1024
        ),
        cost_estimate=pl.CostEstimate(
            flops=40 * layers * depth * width, bytes_accessed=12 * layers * depth * width, transcendentals=0
        ),
    )(fragment_local.reshape(4 * rows, width), anchor.reshape(4 * rows, width), grad)


def outer_step_kernel(mean_ref, anchor_ref, momentum_ref, prev_ref, delta_ref, new_momentum_ref, new_anchor_ref):
    delta_ref[...] = mean_ref[...]
    prev = prev_ref[...]
    momentum = outer_mu * momentum_ref[...] + prev
    new_momentum_ref[...] = momentum
    new_anchor_ref[...] = anchor_ref[...] - outer_rate * (prev + outer_mu * momentum)


def outer_step(mean, anchor, outer_momentum, outer_prev):
    rows, width = mean.shape
    tall = math.gcd(rows, 256)
    spec = pl.BlockSpec((tall, width), lambda i: (i, 0))
    flat = jax.ShapeDtypeStruct(mean.shape, jnp.float32)
    results = pl.pallas_call(
        outer_step_kernel,
        grid=(rows // tall,),
        in_specs=[spec] * 4,
        out_specs=(spec,) * 3,
        out_shape=(flat,) * 3,
        compiler_params=pltpu.CompilerParams(vmem_limit_bytes=32 * 1024 * 1024),
    )(mean, *(a.reshape(mean.shape) for a in (anchor, outer_momentum, outer_prev)))
    return tuple(a.reshape(anchor.shape) for a in results)


def body(
    inputs,
    out_grad,
    inner_weight,
    adam_first,
    adam_second,
    fragment_local,
    anchor,
    outer_momentum,
    outer_prev,
):
    groups = lax.axis_size("fsdp")
    feature_rows = inner_weight.shape[1]
    out_features = inner_weight.shape[2]
    grad = lax.dot_general(
        inputs, out_grad, (((0,), (0,)), ((), ())), preferred_element_type=jnp.float32
    )
    joint = fits(anchor, grad, feature_rows)
    if joint:
        mean, grad_shard, squares = joint_sums(anchor, fragment_local, grad, feature_rows)
        norm_sq = jnp.sum(squares)
    else:
        grad_shard = lax.psum_scatter(grad, "fsdp", scatter_dimension=0, tiled=True)
        norm_sq = lax.psum(jnp.sum(grad_shard * grad_shard), "fsdp")
    clip_limit = clip_rms * math.sqrt(feature_rows * groups * out_features)
    factor = jnp.minimum(1.0, clip_limit / jnp.sqrt(norm_sq + norm_eps))
    clipped = (grad_shard * factor)[None]
    new_first = first_decay * adam_first + (1.0 - first_decay) * clipped
    new_second = second_decay * adam_second + (1.0 - second_decay) * clipped * clipped
    new_weight = inner_weight - inner_rate * new_first / (jnp.sqrt(new_second) + adam_eps)
    if joint:
        outer_delta, new_momentum, new_anchor = outer_step(mean, anchor, outer_momentum, outer_prev)
    else:
        new_momentum = outer_mu * outer_momentum + outer_prev
        new_anchor = anchor - outer_rate * (outer_prev + outer_mu * new_momentum)
        spread = anchor - fragment_local[0]
        outer_delta = lax.psum(spread, "replica") / lax.axis_size("replica")
    return (new_weight, new_first, new_second, outer_delta, new_momentum, new_anchor)


def solution(mesh):
    placed = (
        P(("replica", "fsdp"), None),
        P(("replica", "fsdp"), None),
        P("replica", "fsdp", None),
        P("replica", "fsdp", None),
        P("replica", "fsdp", None),
        P("replica", None, "fsdp", None),
        P(None, "fsdp", None),
        P(None, "fsdp", None),
        P(None, "fsdp", None),
    )
    return jax.shard_map(
        body,
        mesh=mesh,
        in_specs=placed,
        out_specs=(
            P("replica", "fsdp", None),
            P("replica", "fsdp", None),
            P("replica", "fsdp", None),
            P(None, "fsdp", None),
            P(None, "fsdp", None),
            P(None, "fsdp", None),
        ),
        check_vma=False,
    )
```

```python
import functools
import math

import jax
import jax.numpy as jnp
from jax import lax
from jax.experimental import pallas as pl
from jax.experimental.pallas import tpu as pltpu
from jax.sharding import PartitionSpec as P

first_decay = 0.9
second_decay = 0.95
inner_rate = 0.02
outer_rate = 0.7
outer_mu = 0.9
clip_rms = 4.0
adam_eps = 1e-08
norm_eps = 1e-06


KIND_A, KIND_B, KIND_C, KIND_G0, KIND_G1, KIND_F = range(6)
SPAN = 172.0
HALF_SPAN = 86.0
PIECES = 2
STEP_ROWS = 32


def outer_kernel(
    rows,
    width,
    group,
    local_ref,
    anchor_ref,
    inputs_ref,
    out_grad_ref,
    out_ref,
    shard_ref,
    norm_ref,
    vf,
    va,
    sent,
    held,
    load_sem,
    store_sem,
    send_sem,
    recv_sem,
    own,
    other,
    twin,
    grad_sent,
    grad_held,
    part_sent,
    part_held,
    shard_sem,
    twin_sem,
    grad_sem,
    part_sem,
):
    me = lax.axis_index("replica")
    ny = (me + 2) % 4
    nx = 3 - ny
    diag = 3 - me
    neighbour = (nx, ny)
    owners = (diag, nx, ny, me)
    steps = rows // STEP_ROWS

    place = lax.axis_index("fsdp")
    core = place % 2
    chip = place // 2
    chips = group // 2
    block = shard_ref.shape[0]
    grad_steps = block // STEP_ROWS

    def term(s, owner_core):
        start = pl.multiple_of((((chip + s) % chips) * 2 + owner_core) * block, block)
        return lax.dot_general(
            inputs_ref[:, pl.ds(start, block)],
            out_grad_ref[...],
            (((0,), (0,)), ((), ())),
            preferred_element_type=jnp.float32,
        )

    def twin_copy(s):
        return pltpu.make_async_remote_copy(
            src_ref=other.at[s],
            dst_ref=twin.at[s],
            send_sem=twin_sem.at[0, s],
            recv_sem=twin_sem.at[1, s],
            device_id={"fsdp": chip * 2 + 1 - core},
            device_id_type=pl.DeviceIdType.MESH,
        )

    def grad_copy(s):
        return pltpu.make_async_remote_copy(
            src_ref=grad_sent.at[s - 1],
            dst_ref=grad_held.at[s - 1],
            send_sem=grad_sem.at[0, s - 1],
            recv_sem=grad_sem.at[1, s - 1],
            device_id={"fsdp": ((chip + s) % chips) * 2 + core},
            device_id_type=pl.DeviceIdType.MESH,
        )

    def part_copy(s):
        return pltpu.make_async_remote_copy(
            src_ref=part_sent,
            dst_ref=part_held.at[s - 1],
            send_sem=part_sem.at[0, s - 1],
            recv_sem=part_sem.at[1, s - 1],
            device_id={"fsdp": (place + s) % group},
            device_id_type=pl.DeviceIdType.MESH,
        )

    loads = []
    for j in range(4):
        part = pl.ds(pl.multiple_of(owners[j] * rows, rows), rows)
        loads.append(
            (
                pltpu.make_async_copy(local_ref.at[part, :], vf.at[j], load_sem.at[j, 0]),
                pltpu.make_async_copy(anchor_ref.at[part, :], va.at[j], load_sem.at[j, 1]),
            )
        )
    for pair in loads:
        for load in pair:
            load.start()

    barrier = pltpu.get_barrier_semaphore()
    for n in neighbour:
        pl.semaphore_signal(barrier, inc=1, device_id={"replica": n}, device_id_type=pl.DeviceIdType.MESH)
    for s in range(1, group):
        pl.semaphore_signal(
            barrier, inc=1, device_id={"fsdp": (place + s) % group}, device_id_type=pl.DeviceIdType.MESH
        )
    pl.semaphore_wait(barrier, group + 1)

    def columns(half, k):
        return pl.ds((half * PIECES + k) * width, width)

    def copy(kind, way, k):
        if kind == KIND_F:
            src = held.at[KIND_G1 if way == 0 else KIND_G0, 1 - way, k]
        elif kind in (KIND_G0, KIND_G1):
            src = sent.at[kind, 0, k]
        else:
            src = sent.at[kind, way, k]
        return pltpu.make_async_remote_copy(
            src_ref=src,
            dst_ref=held.at[kind, way, k],
            send_sem=send_sem.at[kind, way, k],
            recv_sem=recv_sem.at[kind, way, k],
            device_id={"replica": neighbour[way]},
            device_id_type=pl.DeviceIdType.MESH,
        )

    def scale_of(box, kind, way, k):
        return box[kind, way, k, rows : rows + 16, :].astype(jnp.float32)[0:1] * (1.0 / SPAN)

    def decoded(box, kind, way, k, scale, r):
        code = box[kind, way, k, r, :].astype(jnp.float32)
        size = (jnp.log(jnp.abs(code)) + HALF_SPAN) * scale
        return jnp.where(code < 0.0, -size, size)

    def encode(j, half, k, kind, way, terms, factor=None):
        cs = columns(half, k)
        scales = [scale_of(held, t[0], t[1], k) for t in terms]

        def gather(i, top):
            r = pl.ds(pl.multiple_of(i * STEP_ROWS, STEP_ROWS), STEP_ROWS)
            x = va[j, r, cs] - vf[j, r, cs]
            for t, s in zip(terms, scales):
                x = x + decoded(held, t[0], t[1], k, s, r)
            if factor is not None:
                x = x * factor
            vf[j, r, cs] = x
            return jnp.maximum(top, jnp.max(jnp.abs(x).reshape(STEP_ROWS // 8, 8, width), axis=0))

        top = lax.fori_loop(0, steps, gather, jnp.zeros((8, width), jnp.float32))
        top = (jnp.max(top, axis=0, keepdims=True) * 1.01 + 1e-30).astype(jnp.bfloat16)
        sent[kind, way, k, rows : rows + 16, :] = jnp.broadcast_to(top.astype(jnp.float32), (16, width)).astype(
            jnp.bfloat16
        )
        slope = SPAN / top.astype(jnp.float32)

        def write(i, c):
            r = pl.ds(pl.multiple_of(i * STEP_ROWS, STEP_ROWS), STEP_ROWS)
            x = vf[j, r, cs]
            y = jnp.exp(jnp.abs(x) * slope - HALF_SPAN)
            sent[kind, way, k, r, :] = jnp.where(x < 0.0, -y, y).astype(jnp.bfloat16)
            return c

        lax.fori_loop(0, steps, write, 0)

    def unfold(j, half, k, box, kind, way):
        cs = columns(half, k)
        scale = scale_of(box, kind, way, k)

        def step(i, c):
            r = pl.ds(pl.multiple_of(i * STEP_ROWS, STEP_ROWS), STEP_ROWS)
            vf[j, r, cs] = decoded(box, kind, way, k, scale, r)
            return c

        lax.fori_loop(0, steps, step, 0)

    def loaded(j):
        for load in loads[j]:
            load.wait()

    def encode_grad(s):
        span = own.shape[2]

        def gather(i, top):
            r = pl.ds(pl.multiple_of(i * STEP_ROWS, STEP_ROWS), STEP_ROWS)
            x = own[s, r, :] + twin[s, r, :]
            own[s, r, :] = x
            return jnp.maximum(top, jnp.max(jnp.abs(x).reshape(STEP_ROWS // 8, 8, span), axis=0))

        top = lax.fori_loop(0, grad_steps, gather, jnp.zeros((8, span), jnp.float32))
        top = (jnp.max(top, axis=0, keepdims=True) * 1.01 + 1e-30).astype(jnp.bfloat16).astype(jnp.float32)
        grad_sent[s - 1, block : block + 16, :] = jnp.broadcast_to(top, (16, span)).astype(jnp.bfloat16)
        slope = SPAN / top

        def write(i, c):
            r = pl.ds(pl.multiple_of(i * STEP_ROWS, STEP_ROWS), STEP_ROWS)
            x = own[s, r, :]
            y = jnp.exp(jnp.abs(x) * slope - HALF_SPAN)
            grad_sent[s - 1, r, :] = jnp.where(x < 0.0, -y, y).astype(jnp.bfloat16)
            return c

        lax.fori_loop(0, grad_steps, write, 0)

    def reduce_grad():
        span = own.shape[2]
        scales = [
            grad_held[s - 1, block : block + 16, :].astype(jnp.float32)[0:1] * (1.0 / SPAN)
            for s in range(1, chips)
        ]

        def step(i, squares):
            r = pl.ds(pl.multiple_of(i * STEP_ROWS, STEP_ROWS), STEP_ROWS)
            x = own[0, r, :] + twin[0, r, :]
            for s in range(1, chips):
                code = grad_held[s - 1, r, :].astype(jnp.float32)
                size = (jnp.log(jnp.abs(code)) + HALF_SPAN) * scales[s - 1]
                x = x + jnp.where(code < 0.0, -size, size)
            own[0, r, :] = x
            return squares + jnp.sum((x * x).reshape(STEP_ROWS // 8, 8, span), axis=0)

        squares = lax.fori_loop(0, grad_steps, step, jnp.zeros((8, span), jnp.float32))
        total = squares[:, 0:128]
        for c in range(1, span // 128):
            total = total + squares[:, c * 128 : (c + 1) * 128]
        part_sent[...] = total

    loaded(0)
    for k in range(PIECES):
        for way in (0, 1):
            encode(0, 1 - way, k, KIND_A, way, ())
            copy(KIND_A, way, k).start()
    farthest_first = (2, 1, 3, 0) if chips == 4 else (*range(1, chips), 0)
    for s in farthest_first:
        other[s, :, :] = term(s, 1 - core)
        twin_copy(s).start()
    loaded(1)
    loaded(2)
    for k in range(PIECES):
        for way in (0, 1):
            encode(1 + way, 1 - way, k, KIND_B, way, ())
            copy(KIND_B, way, k).start()
    for s in farthest_first:
        own[s, :, :] = term(s, core)
    for s in farthest_first[:-1]:
        twin_copy(s).wait_recv()
        encode_grad(s)
        grad_copy(s).start()
    for k in range(PIECES):
        for way in (0, 1):
            copy(KIND_A, 1 - way, k).wait_recv()
            encode(1 + way, way, k, KIND_C, way, ((KIND_A, 1 - way),))
            copy(KIND_C, way, k).start()
    loaded(3)
    for k in range(PIECES):
        for half in (0, 1):
            copy(KIND_B, 1 - half, k).wait_recv()
            copy(KIND_C, half, k).wait_recv()
            encode(3, half, k, KIND_G0 + half, 0, ((KIND_B, 1 - half), (KIND_C, half)), 0.25)
            for way in (0, 1):
                copy(KIND_G0 + half, way, k).start()

    twin_copy(0).wait_recv()
    for s in range(1, chips):
        grad_copy(s).wait_recv()
    reduce_grad()
    for s in range(1, group):
        part_copy(s).start()
    shard_store = pltpu.make_async_copy(own.at[0], shard_ref, shard_sem)
    shard_store.start()

    def store(j):
        part = pl.ds(pl.multiple_of(owners[j] * rows, rows), rows)
        return pltpu.make_async_copy(vf.at[j], out_ref.at[part, :], store_sem.at[j])

    for k in range(PIECES):
        for half in (0, 1):
            unfold(3, half, k, sent, KIND_G0 + half, 0)
    store(3).start()
    for k in range(PIECES):
        for way in (0, 1):
            first = KIND_G1 if way == 0 else KIND_G0
            copy(first, 1 - way, k).wait_recv()
            copy(KIND_F, way, k).start()
    for k in range(PIECES):
        for way in (0, 1):
            unfold(1 + way, way, k, held, KIND_G0 + way, way)
    for way in (0, 1):
        for k in range(PIECES):
            late = 1 - way
            copy(KIND_G0 + late, way, k).wait_recv()
            unfold(1 + way, late, k, held, KIND_G0 + late, way)
        store(1 + way).start()
    for k in range(PIECES):
        for way in (0, 1):
            copy(KIND_F, way, k).wait_recv()
            unfold(0, 1 - way, k, held, KIND_F, way)
    store(0).start()
    norm = part_sent[...]
    for s in range(1, group):
        part_copy(s).wait_recv()
        norm = norm + part_held[s - 1]
    norm_ref[...] = norm
    shard_store.wait()
    for s in range(chips):
        twin_copy(s).wait_send()
    for s in range(1, chips):
        grad_copy(s).wait_send()
    for s in range(1, group):
        part_copy(s).wait_send()
    for kind in range(6):
        for way in (0, 1):
            for k in range(PIECES):
                copy(kind, way, k).wait_send()
    for j in range(4):
        store(j).wait()


def fits(anchor, out_grad, feature_rows):
    layers, depth, width = anchor.shape
    return (
        lax.axis_size("replica") == 4
        and (layers * depth) % (4 * STEP_ROWS) == 0
        and width % (256 * PIECES) == 0
        and lax.axis_size("fsdp") == 8
        and feature_rows % STEP_ROWS == 0
        and out_grad.shape[1] % 128 == 0
        and layers * depth * width <= 2 * 1024 * 1024
    )


def joint_sums(anchor, fragment_local, inputs, out_grad, feature_rows):
    layers, depth, width = anchor.shape
    group = lax.axis_size("fsdp")
    chips = group // 2
    rows = layers * depth // 4
    piece = width // (2 * PIECES)
    out_features = out_grad.shape[1]
    sems = pltpu.SemaphoreType.DMA
    return pl.pallas_call(
        functools.partial(outer_kernel, rows, piece, group),
        out_shape=(
            jax.ShapeDtypeStruct((4 * rows, width), jnp.float32),
            jax.ShapeDtypeStruct((feature_rows, out_features), jnp.float32),
            jax.ShapeDtypeStruct((8, 128), jnp.float32),
        ),
        in_specs=[pl.BlockSpec(memory_space=pl.ANY)] * 2 + [pl.BlockSpec(memory_space=pltpu.VMEM)] * 2,
        out_specs=(
            pl.BlockSpec(memory_space=pl.ANY),
            pl.BlockSpec(memory_space=pl.ANY),
            pl.BlockSpec(memory_space=pltpu.VMEM),
        ),
        scratch_shapes=[
            pltpu.VMEM((4, rows, width), jnp.float32),
            pltpu.VMEM((4, rows, width), jnp.float32),
            pltpu.VMEM((5, 2, PIECES, rows + 16, piece), jnp.bfloat16),
            pltpu.VMEM((6, 2, PIECES, rows + 16, piece), jnp.bfloat16),
            sems((4, 2)),
            sems((4,)),
            sems((6, 2, PIECES)),
            sems((6, 2, PIECES)),
            pltpu.VMEM((chips, feature_rows, out_features), jnp.float32),
            pltpu.VMEM((chips, feature_rows, out_features), jnp.float32),
            pltpu.VMEM((chips, feature_rows, out_features), jnp.float32),
            pltpu.VMEM((chips - 1, feature_rows + 16, out_features), jnp.bfloat16),
            pltpu.VMEM((chips - 1, feature_rows + 16, out_features), jnp.bfloat16),
            pltpu.VMEM((8, 128), jnp.float32),
            pltpu.VMEM((group - 1, 8, 128), jnp.float32),
            sems,
            sems((2, chips)),
            sems((2, chips - 1)),
            sems((2, group - 1)),
        ],
        compiler_params=pltpu.CompilerParams(
            collective_id=0, has_side_effects=True, vmem_limit_bytes=46 * 1024 * 1024
        ),
        cost_estimate=pl.CostEstimate(
            flops=40 * layers * depth * width, bytes_accessed=12 * layers * depth * width, transcendentals=0
        ),
    )(fragment_local.reshape(4 * rows, width), anchor.reshape(4 * rows, width), inputs, out_grad)


def outer_step_kernel(mean_ref, anchor_ref, momentum_ref, prev_ref, delta_ref, new_momentum_ref, new_anchor_ref):
    delta_ref[...] = mean_ref[...]
    prev = prev_ref[...]
    momentum = outer_mu * momentum_ref[...] + prev
    new_momentum_ref[...] = momentum
    new_anchor_ref[...] = anchor_ref[...] - outer_rate * (prev + outer_mu * momentum)


def outer_step(mean, anchor, outer_momentum, outer_prev):
    rows, width = mean.shape
    tall = math.gcd(rows, 256)
    spec = pl.BlockSpec((tall, width), lambda i: (i, 0))
    flat = jax.ShapeDtypeStruct(mean.shape, jnp.float32)
    results = pl.pallas_call(
        outer_step_kernel,
        grid=(rows // tall,),
        in_specs=[spec] * 4,
        out_specs=(spec,) * 3,
        out_shape=(flat,) * 3,
        compiler_params=pltpu.CompilerParams(vmem_limit_bytes=58 * 1024 * 1024),
    )(mean, *(a.reshape(mean.shape) for a in (anchor, outer_momentum, outer_prev)))
    return tuple(a.reshape(anchor.shape) for a in results)


def body(
    inputs,
    out_grad,
    inner_weight,
    adam_first,
    adam_second,
    fragment_local,
    anchor,
    outer_momentum,
    outer_prev,
):
    groups = lax.axis_size("fsdp")
    feature_rows = inner_weight.shape[1]
    out_features = inner_weight.shape[2]
    joint = fits(anchor, out_grad, feature_rows)
    if joint:
        mean, grad_shard, squares = joint_sums(anchor, fragment_local, inputs, out_grad, feature_rows)
        norm_sq = jnp.sum(squares)
    else:
        grad = lax.dot_general(
            inputs, out_grad, (((0,), (0,)), ((), ())), preferred_element_type=jnp.float32
        )
        grad_shard = lax.psum_scatter(grad, "fsdp", scatter_dimension=0, tiled=True)
        norm_sq = lax.psum(jnp.sum(grad_shard * grad_shard), "fsdp")
    clip_limit = clip_rms * math.sqrt(feature_rows * groups * out_features)
    factor = jnp.minimum(1.0, clip_limit / jnp.sqrt(norm_sq + norm_eps))
    clipped = (grad_shard * factor)[None]
    new_first = first_decay * adam_first + (1.0 - first_decay) * clipped
    new_second = second_decay * adam_second + (1.0 - second_decay) * clipped * clipped
    new_weight = inner_weight - inner_rate * new_first / (jnp.sqrt(new_second) + adam_eps)
    if joint:
        outer_delta, new_momentum, new_anchor = outer_step(mean, anchor, outer_momentum, outer_prev)
    else:
        new_momentum = outer_mu * outer_momentum + outer_prev
        new_anchor = anchor - outer_rate * (outer_prev + outer_mu * new_momentum)
        spread = anchor - fragment_local[0]
        outer_delta = lax.psum(spread, "replica") / lax.axis_size("replica")
    return (new_weight, new_first, new_second, outer_delta, new_momentum, new_anchor)


def solution(mesh):
    placed = (
        P(("replica", "fsdp"), None),
        P(("replica", "fsdp"), None),
        P("replica", "fsdp", None),
        P("replica", "fsdp", None),
        P("replica", "fsdp", None),
        P("replica", None, "fsdp", None),
        P(None, "fsdp", None),
        P(None, "fsdp", None),
        P(None, "fsdp", None),
    )
    return jax.shard_map(
        body,
        mesh=mesh,
        in_specs=placed,
        out_specs=(
            P("replica", "fsdp", None),
            P("replica", "fsdp", None),
            P("replica", "fsdp", None),
            P(None, "fsdp", None),
            P(None, "fsdp", None),
            P(None, "fsdp", None),
        ),
        check_vma=False,
    )
```

```python
import functools
import math

import jax
import jax.numpy as jnp
from jax import lax
from jax.experimental import pallas as pl
from jax.experimental.pallas import tpu as pltpu
from jax.sharding import PartitionSpec as P

first_decay = 0.9
second_decay = 0.95
inner_rate = 0.02
outer_rate = 0.7
outer_mu = 0.9
clip_rms = 4.0
adam_eps = 1e-08
norm_eps = 1e-06


KIND_A, KIND_B, KIND_C, KIND_G0, KIND_G1, KIND_F = range(6)
SPAN = 172.0
HALF_SPAN = 86.0
PIECES = 2
STEP_ROWS = 32


def outer_kernel(
    rows,
    width,
    group,
    local_ref,
    anchor_ref,
    inputs_ref,
    out_grad_ref,
    out_ref,
    shard_ref,
    norm_ref,
    va,
    sent,
    held,
    load_sem,
    send_sem,
    recv_sem,
    own,
    other,
    twin,
    grad_sent,
    grad_held,
    part_sent,
    part_held,
    shard_sem,
    twin_sem,
    grad_sem,
    part_sem,
):
    me = lax.axis_index("replica")
    ny = (me + 2) % 4
    nx = 3 - ny
    diag = 3 - me
    neighbour = (nx, ny)
    owners = (diag, nx, ny, me)
    steps = rows // STEP_ROWS

    place = lax.axis_index("fsdp")
    core = place % 2
    chip = place // 2
    chips = group // 2
    block = shard_ref.shape[0]
    grad_steps = block // STEP_ROWS

    def term(s, owner_core):
        start = pl.multiple_of((((chip + s) % chips) * 2 + owner_core) * block, block)
        return lax.dot_general(
            inputs_ref[:, pl.ds(start, block)],
            out_grad_ref[...],
            (((0,), (0,)), ((), ())),
            preferred_element_type=jnp.float32,
        )

    def twin_copy(s):
        return pltpu.make_async_remote_copy(
            src_ref=other.at[s],
            dst_ref=twin.at[s],
            send_sem=twin_sem.at[0, s],
            recv_sem=twin_sem.at[1, s],
            device_id={"fsdp": chip * 2 + 1 - core},
            device_id_type=pl.DeviceIdType.MESH,
        )

    def grad_copy(s):
        return pltpu.make_async_remote_copy(
            src_ref=grad_sent.at[s - 1],
            dst_ref=grad_held.at[s - 1],
            send_sem=grad_sem.at[0, s - 1],
            recv_sem=grad_sem.at[1, s - 1],
            device_id={"fsdp": ((chip + s) % chips) * 2 + core},
            device_id_type=pl.DeviceIdType.MESH,
        )

    def part_copy(s):
        return pltpu.make_async_remote_copy(
            src_ref=part_sent,
            dst_ref=part_held.at[s - 1],
            send_sem=part_sem.at[0, s - 1],
            recv_sem=part_sem.at[1, s - 1],
            device_id={"fsdp": (place + s) % group},
            device_id_type=pl.DeviceIdType.MESH,
        )

    loads = []
    for j in range(4):
        part = pl.ds(pl.multiple_of(owners[j] * rows, rows), rows)
        loads.append(
            (
                pltpu.make_async_copy(local_ref.at[part, :], out_ref.at[part, :], load_sem.at[j, 0]),
                pltpu.make_async_copy(anchor_ref.at[part, :], va.at[j], load_sem.at[j, 1]),
            )
        )
    for pair in loads:
        for load in pair:
            load.start()

    barrier = pltpu.get_barrier_semaphore()
    for n in neighbour:
        pl.semaphore_signal(barrier, inc=1, device_id={"replica": n}, device_id_type=pl.DeviceIdType.MESH)
    for s in range(1, group):
        pl.semaphore_signal(
            barrier, inc=1, device_id={"fsdp": (place + s) % group}, device_id_type=pl.DeviceIdType.MESH
        )
    pl.semaphore_wait(barrier, group + 1)

    def spot(j, i):
        return pl.ds(pl.multiple_of(owners[j] * rows + i * STEP_ROWS, STEP_ROWS), STEP_ROWS)

    def columns(half, k):
        return pl.ds((half * PIECES + k) * width, width)

    def copy(kind, way, k):
        if kind == KIND_F:
            src = held.at[KIND_G1 if way == 0 else KIND_G0, 1 - way, k]
        elif kind in (KIND_G0, KIND_G1):
            src = sent.at[kind, 0, k]
        else:
            src = sent.at[kind, way, k]
        return pltpu.make_async_remote_copy(
            src_ref=src,
            dst_ref=held.at[kind, way, k],
            send_sem=send_sem.at[kind, way, k],
            recv_sem=recv_sem.at[kind, way, k],
            device_id={"replica": neighbour[way]},
            device_id_type=pl.DeviceIdType.MESH,
        )

    def scale_of(box, kind, way, k):
        return box[kind, way, k, rows : rows + 16, :].astype(jnp.float32)[0:1] * (1.0 / SPAN)

    def decoded(box, kind, way, k, scale, r):
        code = box[kind, way, k, r, :].astype(jnp.float32)
        size = (jnp.log(jnp.abs(code)) + HALF_SPAN) * scale
        return jnp.where(code < 0.0, -size, size)

    def encode(j, half, k, kind, way, terms, factor=None):
        cs = columns(half, k)
        scales = [scale_of(held, t[0], t[1], k) for t in terms]

        def gather(i, top):
            r = pl.ds(pl.multiple_of(i * STEP_ROWS, STEP_ROWS), STEP_ROWS)
            x = va[j, r, cs] - out_ref[spot(j, i), cs]
            for t, s in zip(terms, scales):
                x = x + decoded(held, t[0], t[1], k, s, r)
            if factor is not None:
                x = x * factor
            out_ref[spot(j, i), cs] = x
            return jnp.maximum(top, jnp.max(jnp.abs(x).reshape(STEP_ROWS // 8, 8, width), axis=0))

        top = lax.fori_loop(0, steps, gather, jnp.zeros((8, width), jnp.float32))
        top = (jnp.max(top, axis=0, keepdims=True) * 1.01 + 1e-30).astype(jnp.bfloat16)
        sent[kind, way, k, rows : rows + 16, :] = jnp.broadcast_to(top.astype(jnp.float32), (16, width)).astype(
            jnp.bfloat16
        )
        slope = SPAN / top.astype(jnp.float32)

        def write(i, c):
            r = pl.ds(pl.multiple_of(i * STEP_ROWS, STEP_ROWS), STEP_ROWS)
            x = out_ref[spot(j, i), cs]
            y = jnp.exp(jnp.abs(x) * slope - HALF_SPAN)
            sent[kind, way, k, r, :] = jnp.where(x < 0.0, -y, y).astype(jnp.bfloat16)
            return c

        lax.fori_loop(0, steps, write, 0)

    def unfold(j, half, k, box, kind, way):
        cs = columns(half, k)
        scale = scale_of(box, kind, way, k)

        def step(i, c):
            r = pl.ds(pl.multiple_of(i * STEP_ROWS, STEP_ROWS), STEP_ROWS)
            out_ref[spot(j, i), cs] = decoded(box, kind, way, k, scale, r)
            return c

        lax.fori_loop(0, steps, step, 0)

    def loaded(j):
        for load in loads[j]:
            load.wait()

    def encode_grad(s):
        span = own.shape[2]

        def gather(i, top):
            r = pl.ds(pl.multiple_of(i * STEP_ROWS, STEP_ROWS), STEP_ROWS)
            x = own[s, r, :] + twin[s, r, :]
            own[s, r, :] = x
            return jnp.maximum(top, jnp.max(jnp.abs(x).reshape(STEP_ROWS // 8, 8, span), axis=0))

        top = lax.fori_loop(0, grad_steps, gather, jnp.zeros((8, span), jnp.float32))
        top = (jnp.max(top, axis=0, keepdims=True) * 1.01 + 1e-30).astype(jnp.bfloat16).astype(jnp.float32)
        grad_sent[s - 1, block : block + 16, :] = jnp.broadcast_to(top, (16, span)).astype(jnp.bfloat16)
        slope = SPAN / top

        def write(i, c):
            r = pl.ds(pl.multiple_of(i * STEP_ROWS, STEP_ROWS), STEP_ROWS)
            x = own[s, r, :]
            y = jnp.exp(jnp.abs(x) * slope - HALF_SPAN)
            grad_sent[s - 1, r, :] = jnp.where(x < 0.0, -y, y).astype(jnp.bfloat16)
            return c

        lax.fori_loop(0, grad_steps, write, 0)

    def reduce_grad():
        span = own.shape[2]
        scales = [
            grad_held[s - 1, block : block + 16, :].astype(jnp.float32)[0:1] * (1.0 / SPAN)
            for s in range(1, chips)
        ]

        def step(i, squares):
            r = pl.ds(pl.multiple_of(i * STEP_ROWS, STEP_ROWS), STEP_ROWS)
            x = own[0, r, :] + twin[0, r, :]
            for s in range(1, chips):
                code = grad_held[s - 1, r, :].astype(jnp.float32)
                size = (jnp.log(jnp.abs(code)) + HALF_SPAN) * scales[s - 1]
                x = x + jnp.where(code < 0.0, -size, size)
            own[0, r, :] = x
            return squares + jnp.sum((x * x).reshape(STEP_ROWS // 8, 8, span), axis=0)

        squares = lax.fori_loop(0, grad_steps, step, jnp.zeros((8, span), jnp.float32))
        total = squares[:, 0:128]
        for c in range(1, span // 128):
            total = total + squares[:, c * 128 : (c + 1) * 128]
        part_sent[...] = total

    loaded(0)
    for k in range(PIECES):
        for way in (0, 1):
            encode(0, 1 - way, k, KIND_A, way, ())
            copy(KIND_A, way, k).start()
    farthest_first = (2, 1, 3, 0) if chips == 4 else (*range(1, chips), 0)
    for s in farthest_first:
        other[s, :, :] = term(s, 1 - core)
        twin_copy(s).start()
    loaded(1)
    loaded(2)
    for k in range(PIECES):
        for way in (0, 1):
            encode(1 + way, 1 - way, k, KIND_B, way, ())
            copy(KIND_B, way, k).start()
    for s in farthest_first:
        own[s, :, :] = term(s, core)
    for s in farthest_first[:-1]:
        twin_copy(s).wait_recv()
        encode_grad(s)
        grad_copy(s).start()
    for k in range(PIECES):
        for way in (0, 1):
            copy(KIND_A, 1 - way, k).wait_recv()
            encode(1 + way, way, k, KIND_C, way, ((KIND_A, 1 - way),))
            copy(KIND_C, way, k).start()
    loaded(3)
    for k in range(PIECES):
        for half in (0, 1):
            copy(KIND_B, 1 - half, k).wait_recv()
            copy(KIND_C, half, k).wait_recv()
            encode(3, half, k, KIND_G0 + half, 0, ((KIND_B, 1 - half), (KIND_C, half)), 0.25)
            for way in (0, 1):
                copy(KIND_G0 + half, way, k).start()

    twin_copy(0).wait_recv()
    for s in range(1, chips):
        grad_copy(s).wait_recv()
    reduce_grad()
    for s in range(1, group):
        part_copy(s).start()
    shard_store = pltpu.make_async_copy(own.at[0], shard_ref, shard_sem)
    shard_store.start()

    for k in range(PIECES):
        for half in (0, 1):
            unfold(3, half, k, sent, KIND_G0 + half, 0)
    for k in range(PIECES):
        for way in (0, 1):
            first = KIND_G1 if way == 0 else KIND_G0
            copy(first, 1 - way, k).wait_recv()
            copy(KIND_F, way, k).start()
    for k in range(PIECES):
        for way in (0, 1):
            unfold(1 + way, way, k, held, KIND_G0 + way, way)
    for way in (0, 1):
        for k in range(PIECES):
            late = 1 - way
            copy(KIND_G0 + late, way, k).wait_recv()
            unfold(1 + way, late, k, held, KIND_G0 + late, way)
    for k in range(PIECES):
        for way in (0, 1):
            copy(KIND_F, way, k).wait_recv()
            unfold(0, 1 - way, k, held, KIND_F, way)
    norm = part_sent[...]
    for s in range(1, group):
        part_copy(s).wait_recv()
        norm = norm + part_held[s - 1]
    norm_ref[...] = norm
    shard_store.wait()
    for s in range(chips):
        twin_copy(s).wait_send()
    for s in range(1, chips):
        grad_copy(s).wait_send()
    for s in range(1, group):
        part_copy(s).wait_send()
    for kind in range(6):
        for way in (0, 1):
            for k in range(PIECES):
                copy(kind, way, k).wait_send()


def fits(anchor, out_grad, feature_rows):
    layers, depth, width = anchor.shape
    return (
        lax.axis_size("replica") == 4
        and (layers * depth) % (4 * STEP_ROWS) == 0
        and width % (256 * PIECES) == 0
        and lax.axis_size("fsdp") == 8
        and feature_rows % STEP_ROWS == 0
        and out_grad.shape[1] % 128 == 0
        and layers * depth * width <= 2 * 1024 * 1024
    )


def joint_sums(anchor, fragment_local, inputs, out_grad, feature_rows):
    layers, depth, width = anchor.shape
    group = lax.axis_size("fsdp")
    chips = group // 2
    rows = layers * depth // 4
    piece = width // (2 * PIECES)
    out_features = out_grad.shape[1]
    sems = pltpu.SemaphoreType.DMA
    return pl.pallas_call(
        functools.partial(outer_kernel, rows, piece, group),
        out_shape=(
            jax.ShapeDtypeStruct((4 * rows, width), jnp.float32),
            jax.ShapeDtypeStruct((feature_rows, out_features), jnp.float32),
            jax.ShapeDtypeStruct((8, 128), jnp.float32),
        ),
        in_specs=[pl.BlockSpec(memory_space=pl.ANY)] * 2 + [pl.BlockSpec(memory_space=pltpu.VMEM)] * 2,
        out_specs=(
            pl.BlockSpec(memory_space=pltpu.VMEM),
            pl.BlockSpec(memory_space=pl.ANY),
            pl.BlockSpec(memory_space=pltpu.VMEM),
        ),
        scratch_shapes=[
            pltpu.VMEM((4, rows, width), jnp.float32),
            pltpu.VMEM((5, 2, PIECES, rows + 16, piece), jnp.bfloat16),
            pltpu.VMEM((6, 2, PIECES, rows + 16, piece), jnp.bfloat16),
            sems((4, 2)),
            sems((6, 2, PIECES)),
            sems((6, 2, PIECES)),
            pltpu.VMEM((chips, feature_rows, out_features), jnp.float32),
            pltpu.VMEM((chips, feature_rows, out_features), jnp.float32),
            pltpu.VMEM((chips, feature_rows, out_features), jnp.float32),
            pltpu.VMEM((chips - 1, feature_rows + 16, out_features), jnp.bfloat16),
            pltpu.VMEM((chips - 1, feature_rows + 16, out_features), jnp.bfloat16),
            pltpu.VMEM((8, 128), jnp.float32),
            pltpu.VMEM((group - 1, 8, 128), jnp.float32),
            sems,
            sems((2, chips)),
            sems((2, chips - 1)),
            sems((2, group - 1)),
        ],
        compiler_params=pltpu.CompilerParams(
            collective_id=0, has_side_effects=True, vmem_limit_bytes=38 * 1024 * 1024
        ),
        cost_estimate=pl.CostEstimate(
            flops=40 * layers * depth * width, bytes_accessed=12 * layers * depth * width, transcendentals=0
        ),
    )(fragment_local.reshape(4 * rows, width), anchor.reshape(4 * rows, width), inputs, out_grad)


def outer_step_kernel(mean_ref, anchor_ref, momentum_ref, prev_ref, delta_ref, new_momentum_ref, new_anchor_ref):
    delta_ref[...] = mean_ref[...]
    prev = prev_ref[...]
    momentum = outer_mu * momentum_ref[...] + prev
    new_momentum_ref[...] = momentum
    new_anchor_ref[...] = anchor_ref[...] - outer_rate * (prev + outer_mu * momentum)


def outer_step(mean, anchor, outer_momentum, outer_prev):
    rows, width = mean.shape
    tall = math.gcd(rows, 128)
    spec = pl.BlockSpec((tall, width), lambda i: (i, 0))
    flat = jax.ShapeDtypeStruct(mean.shape, jnp.float32)
    results = pl.pallas_call(
        outer_step_kernel,
        grid=(rows // tall,),
        in_specs=[spec] * 4,
        out_specs=(spec,) * 3,
        out_shape=(flat,) * 3,
        compiler_params=pltpu.CompilerParams(vmem_limit_bytes=44 * 1024 * 1024),
    )(mean, *(a.reshape(mean.shape) for a in (anchor, outer_momentum, outer_prev)))
    return tuple(a.reshape(anchor.shape) for a in results)


def body(
    inputs,
    out_grad,
    inner_weight,
    adam_first,
    adam_second,
    fragment_local,
    anchor,
    outer_momentum,
    outer_prev,
):
    groups = lax.axis_size("fsdp")
    feature_rows = inner_weight.shape[1]
    out_features = inner_weight.shape[2]
    joint = fits(anchor, out_grad, feature_rows)
    if joint:
        mean, grad_shard, squares = joint_sums(anchor, fragment_local, inputs, out_grad, feature_rows)
        outer_delta, new_momentum, new_anchor = outer_step(mean, anchor, outer_momentum, outer_prev)
        squares, outer_delta = lax.optimization_barrier((squares, outer_delta))
        norm_sq = jnp.sum(squares)
    else:
        grad = lax.dot_general(
            inputs, out_grad, (((0,), (0,)), ((), ())), preferred_element_type=jnp.float32
        )
        grad_shard = lax.psum_scatter(grad, "fsdp", scatter_dimension=0, tiled=True)
        norm_sq = lax.psum(jnp.sum(grad_shard * grad_shard), "fsdp")
    clip_limit = clip_rms * math.sqrt(feature_rows * groups * out_features)
    factor = jnp.minimum(1.0, clip_limit / jnp.sqrt(norm_sq + norm_eps))
    clipped = (grad_shard * factor)[None]
    new_first = first_decay * adam_first + (1.0 - first_decay) * clipped
    new_second = second_decay * adam_second + (1.0 - second_decay) * clipped * clipped
    new_weight = inner_weight - inner_rate * new_first / (jnp.sqrt(new_second) + adam_eps)
    if not joint:
        new_momentum = outer_mu * outer_momentum + outer_prev
        new_anchor = anchor - outer_rate * (outer_prev + outer_mu * new_momentum)
        spread = anchor - fragment_local[0]
        outer_delta = lax.psum(spread, "replica") / lax.axis_size("replica")
    return (new_weight, new_first, new_second, outer_delta, new_momentum, new_anchor)


def solution(mesh):
    placed = (
        P(("replica", "fsdp"), None),
        P(("replica", "fsdp"), None),
        P("replica", "fsdp", None),
        P("replica", "fsdp", None),
        P("replica", "fsdp", None),
        P("replica", None, "fsdp", None),
        P(None, "fsdp", None),
        P(None, "fsdp", None),
        P(None, "fsdp", None),
    )
    return jax.shard_map(
        body,
        mesh=mesh,
        in_specs=placed,
        out_specs=(
            P("replica", "fsdp", None),
            P("replica", "fsdp", None),
            P("replica", "fsdp", None),
            P(None, "fsdp", None),
            P(None, "fsdp", None),
            P(None, "fsdp", None),
        ),
        check_vma=False,
    )
```
